32 devices in a mesh: rep: 4 (over y, core), fsdp: 8 (over z, x).
Axes of the slice: x: 2, y: 2, z: 4, core: 2. Of those that a mesh axis runs over, the one named last changes fastest.
Arguments:
- tokens: bfloat16 [64, 1024, 1024], P(('rep', 'fsdp')), may hold values from -12 to 12
- lengths: int32 [64], P(('rep', 'fsdp')), may hold values from 384 to 1024, as said below
- cotangent: bfloat16 [64, 1024, 1024], P(('rep', 'fsdp')), may hold values from -6 to 6
- mix_weight: bfloat16 [1024, 3072], P('fsdp'), may hold values from -0.25 to 0.25
- mix_bias: bfloat16 [3072], P('fsdp'), may hold values from -1.75 to 1.75
- proj_weight: bfloat16 [1024, 1024], P('fsdp'), may hold values from -1.5 to 1.5
- proj_bias: bfloat16 [1024], P('fsdp'), may hold values from -1.75 to 1.75
- up_weight: bfloat16 [1024, 4096], P('fsdp'), may hold values from -0.1875 to 0.1875
- up_bias: bfloat16 [4096], P('fsdp'), may hold values from -1.75 to 1.75
- down_weight: bfloat16 [4096, 1024], P('fsdp'), may hold values from -0.09375 to 0.09375
- down_bias: bfloat16 [1024], P('fsdp'), may hold values from -1.75 to 1.75
- gain_attn: bfloat16 [1024], P('fsdp'), may hold values from 0.099609375 to 1.8984375
- shift_attn: bfloat16 [1024], P('fsdp'), may hold values from -1.75 to 1.75
- gain_mlp: bfloat16 [1024], P('fsdp'), may hold values from 0.099609375 to 1.8984375
- shift_mlp: bfloat16 [1024], P('fsdp'), may hold values from -1.75 to 1.75
Outputs:
- layer_out: bfloat16 [64, 1024, 1024], P(('rep', 'fsdp'))
- grad_tokens: float32 [64, 1024, 1024], P(('rep', 'fsdp'))
- grad_mix_weight: float32 [1024, 3072], P('fsdp')
- grad_mix_bias: float32 [3072], P('fsdp')
- grad_proj_weight: float32 [1024, 1024], P('fsdp')
- grad_proj_bias: float32 [1024], P('fsdp')
- grad_up_weight: float32 [1024, 4096], P('fsdp')
- grad_up_bias: float32 [4096], P('fsdp')
- grad_down_weight: float32 [4096, 1024], P('fsdp')
- grad_down_bias: float32 [1024], P('fsdp')
- grad_gain_attn: float32 [1024], P('fsdp')
- grad_shift_attn: float32 [1024], P('fsdp')
- grad_gain_mlp: float32 [1024], P('fsdp')
- grad_shift_mlp: float32 [1024], P('fsdp')
The draws below stay inside these ranges and needn't reach their ends.
Inputs may be any that keep to these rules, and one draw needn't show every extreme that they name: `lengths`: the length of each micro-batch's sequence, a multiple of 128; its rows from the length on are padding; at least one micro-batch holds 1024 tokens.
All inputs are finite; a program needn't handle non-finite values.
Results may differ from the reference program's by a relative error of at most 0.017.
Values may be sent and summed in bfloat16 or wider, within the bound.
A program may use at most 512 MiB of HBM per device.

```python
import math
import jax
import jax.numpy as jnp
from jax import lax

D = 1024
FF = 4096
HEADS = 16
HEAD = 64
ROT = 16
SLOT = 1024
SEQS = 64


def draw_lengths(key, part):
    key = jax.random.fold_in(key, 5)
    blocks = jax.random.randint(key, (SEQS,), 3, 9)
    chosen = jax.random.randint(jax.random.fold_in(key, 1), (), 0, SEQS)
    blocks = jnp.where(jnp.arange(SEQS) == chosen, 8, blocks)
    return (blocks * (SLOT // 8)).astype(jnp.int32)


def with_spikes(drawn, own_key, source, target, shards_of, factor):
    owner, partner = [(jnp.arange(drawn.shape[dim]) // (drawn.shape[dim] // shards_of)).reshape([-1 if axis == dim else 1 for axis in range(drawn.ndim)]) for dim in (source, target)]
    chosen = jax.random.permutation(own_key, shards_of)[partner]
    strong = (owner == chosen) | (owner == (partner + shards_of // 2) % shards_of)
    return jnp.where(strong, factor * drawn, drawn)


def shard_levels(stream_key, shape, cuts, smallest, high):
    level, own = 1.0, jax.random.fold_in(stream_key, 6)
    for axis_at, shards_of in cuts:
        draws = jnp.exp(jax.random.uniform(jax.random.fold_in(own, axis_at), (shards_of,), jnp.float32, smallest / len(cuts), high / len(cuts)))
        level = level * jnp.repeat(draws, shape[axis_at] // shards_of).reshape([-1 if axis == axis_at else 1 for axis in range(len(shape))])
    return level


def normal_values(own_key, shape, scale, most, cuts=(), held_as=jnp.bfloat16):
    factor_of = shard_levels(own_key, shape, cuts, -0.22, 0.18) if cuts else 1.0
    drawn = jax.random.normal(own_key, shape, jnp.float32) * scale * factor_of
    return jnp.minimum(jnp.maximum(drawn, -most), most).astype(held_as)


def heavy_noise(rng, shape, width, most, shards, heavy, kind=jnp.bfloat16):
    entries = width * jax.random.normal(rng, shape, jnp.float32)
    if shards:
        entries = entries * shard_levels(rng, shape, shards, -0.22, 0.18)
    return jnp.clip(with_spikes(entries, jax.random.fold_in(rng, 3), *heavy), -most, most).astype(kind)


def setup_inputs(seed: int = 0) -> dict:
    key_list = jax.random.split(jax.random.key(seed), 16)
    tokens = heavy_noise(key_list[0], (SEQS, SLOT, D), 1.0, 12.0, ((0, 32),), (0, 2, 32, 2.75))
    lengths = draw_lengths(jax.random.fold_in(key_list[15], 71), 0)
    cotangent = normal_values(key_list[2], (SEQS, SLOT, D), 1.0, 6.0, ((0, 32),))
    mix_weight = normal_values(key_list[3], (D, 3 * D), (D // 2) ** -0.5, 0.25, ((0, 8),))
    mix_bias = normal_values(key_list[4], (3 * D,), 0.3, 1.75, ((0, 8),))
    proj_weight = normal_values(key_list[5], (D, D), (D // 64) ** -0.5, 1.5, ((0, 8),))
    proj_bias = normal_values(key_list[6], (D,), 0.3, 1.75, ((0, 8),))
    up_weight = normal_values(key_list[7], (D, FF), D ** -0.5, 0.1875, ((0, 8),))
    up_bias = normal_values(key_list[8], (FF,), 0.3, 1.75, ((0, 8),))
    down_weight = normal_values(key_list[9], (FF, D), FF ** -0.5, 0.09375, ((0, 8),))
    down_bias = normal_values(key_list[10], (D,), 0.3, 1.75, ((0, 8),))
    gain_attn = jnp.clip(1.0 + 0.18 * jax.random.normal(key_list[11], (D,), jnp.float32), 0.099609375, 1.8984375).astype(jnp.bfloat16)
    shift_attn = normal_values(key_list[12], (D,), 0.3, 1.75, ((0, 8),))
    gain_mlp = jnp.clip(1.0 + 0.18 * jax.random.normal(key_list[13], (D,), jnp.float32), 0.099609375, 1.8984375).astype(jnp.bfloat16)
    shift_mlp = normal_values(key_list[14], (D,), 0.3, 1.75, ((0, 8),))
    return dict(tokens=tokens, lengths=lengths, cotangent=cotangent, mix_weight=mix_weight, mix_bias=mix_bias, proj_weight=proj_weight, proj_bias=proj_bias, up_weight=up_weight, up_bias=up_bias, down_weight=down_weight, down_bias=down_bias, gain_attn=gain_attn, shift_attn=shift_attn, gain_mlp=gain_mlp, shift_mlp=shift_mlp)


@jax.custom_vjp
def low(v):
    return lax.optimization_barrier(v.astype(jnp.bfloat16)).astype(jnp.float32)

@jax.custom_vjp
def low_back(v):
    return v

def low_keep(v):
    return (low(v), None)

def low_pass(kept, grad):
    return (grad,)

def back_keep(v):
    return (v, None)

def back_low(kept, grad):
    return (low(grad),)
low.defvjp(low_keep, low_pass)
low_back.defvjp(back_keep, back_low)
EPS = 1e-05
BASE = 10000.0
HIGHEST = lax.Precision.HIGHEST

def norm_rows(values, gain, shift):
    mean = lax.optimization_barrier(jnp.mean(values, axis=-1, keepdims=True))
    centred = values - mean
    spread = lax.optimization_barrier(jnp.mean(centred * centred, axis=-1, keepdims=True))
    return centred * lax.rsqrt(spread + EPS) * gain + shift

def angle_tables(rows, rotary):
    half = rotary // 2
    steps = jnp.arange(half, dtype=jnp.float32) * (2.0 / rotary)
    inverse = jnp.exp(-math.log(BASE) * steps)
    places = jnp.arange(rows, dtype=jnp.float32)
    angles = places[:, None] * inverse[None, :]
    return (jnp.cos(angles)[:, None, :], jnp.sin(angles)[:, None, :])

def rotate(values, cosines, sines):
    half = cosines.shape[-1]
    leading = values[..., :half]
    trailing = values[..., half:2 * half]
    return jnp.concatenate([leading * cosines - trailing * sines, trailing * cosines + leading * sines, values[..., 2 * half:]], axis=-1)

def layer(params, inputs, valid):
    mix_weight, mix_bias, proj_weight, proj_bias, up_weight, up_bias, down_weight, down_bias, gain_attn, shift_attn, gain_mlp, shift_mlp = params
    cosines, sines = angle_tables(SLOT, ROT)
    first = low(norm_rows(inputs, gain_attn, shift_attn))
    second = low(norm_rows(inputs, gain_mlp, shift_mlp))
    mixed = low_back(jnp.dot(first, mix_weight, precision=HIGHEST) + mix_bias)
    mixed = mixed.reshape(SLOT, 3, HEADS, HEAD)
    query = low(rotate(mixed[:, 0], cosines, sines) * HEAD ** (-0.5))
    keys = low(rotate(mixed[:, 1], cosines, sines))
    values = low(mixed[:, 2])
    scores = low_back(jnp.einsum('qhd,khd->hqk', query, keys, precision=HIGHEST))
    causal = lax.broadcasted_iota(jnp.int32, (SLOT, SLOT), 0) >= lax.broadcasted_iota(jnp.int32, (SLOT, SLOT), 1)
    scores = jnp.where(causal[None], scores, -1e+30)
    probs = low(jax.nn.softmax(scores, axis=-1))
    context = jnp.einsum('hqk,khd->qhd', probs, values, precision=HIGHEST)
    context = low(low_back(context)).reshape(SLOT, HEADS * HEAD)
    attend = jnp.dot(context, proj_weight, precision=HIGHEST) + proj_bias
    hidden = low_back(jnp.dot(second, up_weight, precision=HIGHEST) + up_bias)
    active = low(jax.nn.gelu(hidden, approximate=False))
    feed = jnp.dot(active, down_weight, precision=HIGHEST) + down_bias
    return valid[:, None] * (inputs + attend + feed)

def reference(tokens, lengths, cotangent, mix_weight, mix_bias, proj_weight, proj_bias, up_weight, up_bias, down_weight, down_bias, gain_attn, shift_attn, gain_mlp, shift_mlp):
    params = tuple((item.astype(jnp.float32) for item in (mix_weight, mix_bias, proj_weight, proj_bias, up_weight, up_bias, down_weight, down_bias, gain_attn, shift_attn, gain_mlp, shift_mlp)))
    places = jnp.arange(SLOT, dtype=jnp.int32)
    valid_all = (places[None, :] < lengths[:, None]).astype(jnp.float32)
    inputs = tokens.astype(jnp.float32)

    def whole(weights, rows):

        def single(pair):
            return layer(weights, pair[0], pair[1])
        return lax.map(jax.checkpoint(single), (rows, valid_all))
    outputs, pull = jax.vjp(whole, params, inputs)
    grads, grad_inputs = pull(cotangent.astype(jnp.float32))
    return (outputs.astype(jnp.bfloat16), grad_inputs, grads[0], grads[1], grads[2], grads[3], grads[4], grads[5], grads[6], grads[7], grads[8], grads[9], grads[10], grads[11])
```

```python
import math

import jax
import jax.numpy as jnp
from jax import lax
from jax.experimental import pallas as pl
from jax.experimental.pallas import tpu as pltpu
from jax.sharding import PartitionSpec as P

HEADS = 16
HEAD = 64
ROT = 16
PAIR = 2 * HEAD
GROUPS = 2
QTILE = 256
VMEM = 48 * 1024 * 1024
EPS = 1e-05
BASE = 10000.0
F32 = jnp.float32
BF16 = jnp.bfloat16


def dot_nn(a, b):
    return lax.dot_general(a, b, (((1,), (0,)), ((), ())), preferred_element_type=F32)


def dot_nt(a, b):
    return lax.dot_general(a, b, (((1,), (1,)), ((), ())), preferred_element_type=F32)


def dot_tn(a, b):
    return lax.dot_general(a, b, (((0,), (0,)), ((), ())), preferred_element_type=F32)


def rotary_tables(rows):
    half = ROT // 2
    lane = jnp.arange(PAIR, dtype=jnp.int32) % HEAD
    steps = (lane % half).astype(F32) * (2.0 / ROT)
    inverse = jnp.exp(-math.log(BASE) * steps)
    angles = jnp.arange(rows, dtype=F32)[:, None] * inverse[None, :]
    cosines = jnp.where(lane[None] < ROT, jnp.cos(angles), 1.0)
    ahead = jnp.where(lane[None] < half, -jnp.sin(angles), 0.0)
    behind = jnp.where((lane[None] >= half) & (lane[None] < ROT), jnp.sin(angles), 0.0)
    return cosines, ahead, behind


def mlp_kernel(second, outer, up, up_bias, down, active, grad_hidden):
    hidden = dot_nn(second[...], up[...]) + up_bias[...].astype(F32)
    grad_active = dot_nt(outer[...], down[...])
    below = 0.5 + 0.5 * lax.erf(hidden * (0.5**0.5))
    density = jnp.exp(-0.5 * hidden * hidden) * (1.0 / math.sqrt(2.0 * math.pi))
    active[...] = (hidden * below).astype(BF16)
    grad_hidden[...] = (grad_active * (below + hidden * density)).astype(BF16)


def mlp_front(second, outer, up, up_bias, down):
    rows, width = second.shape
    wide = up.shape[1]
    rt, ft = min(512, rows), min(512, wide)
    out = jax.ShapeDtypeStruct((rows, wide), BF16)
    return pl.pallas_call(
        mlp_kernel,
        grid=(wide // ft, rows // rt),
        in_specs=[
            pl.BlockSpec((rt, width), lambda f, r: (r, 0)),
            pl.BlockSpec((rt, width), lambda f, r: (r, 0)),
            pl.BlockSpec((width, ft), lambda f, r: (0, f)),
            pl.BlockSpec((1, ft), lambda f, r: (0, f)),
            pl.BlockSpec((ft, width), lambda f, r: (f, 0)),
        ],
        out_specs=[pl.BlockSpec((rt, ft), lambda f, r: (r, f))] * 2,
        out_shape=[out, out],
        compiler_params=pltpu.CompilerParams(vmem_limit_bytes=VMEM),
        cost_estimate=pl.CostEstimate(
            flops=4 * rows * width * wide,
            bytes_accessed=rows * wide * 4 + width * wide * 4 + rows * width * 32,
            transcendentals=2 * rows * wide,
        ),
    )(second, outer, up, up_bias.reshape(1, wide), down)


def attention_kernel(qin, kin, vin, gin, cosines, ahead, behind, context, gq, gk, gv, acc_k, acc_v):
    rows = qin.shape[1]
    cos, s1, s2 = cosines[...], ahead[...], behind[...]

    def turn(u):
        return u * cos + pltpu.roll(u, PAIR - ROT // 2, 1) * s1 + pltpu.roll(u, ROT // 2, 1) * s2

    def back(u, c, a, b):
        return u * c - pltpu.roll(u, PAIR - ROT // 2, 1) * a - pltpu.roll(u, ROT // 2, 1) * b

    query = (turn(qin[0]) * HEAD ** (-0.5)).astype(BF16)
    keys = turn(kin[0]).astype(BF16)
    values = vin[0].astype(BF16)
    grad = gin[0]
    lane = lax.broadcasted_iota(jnp.int32, (1, PAIR), 1)
    causal = lax.broadcasted_iota(jnp.int32, (QTILE, QTILE), 0) >= lax.broadcasted_iota(
        jnp.int32, (QTILE, QTILE), 1
    )
    zero = jnp.zeros((), BF16)
    halves = [(lane < HEAD), (lane >= HEAD)]
    query_h = [jnp.where(m, query, zero) for m in halves]
    keys_h = [jnp.where(m, keys, zero) for m in halves]
    values_h = [jnp.where(m, values, zero) for m in halves]
    grad_h = [jnp.where(m, grad, zero) for m in halves]
    acc_k[...] = jnp.zeros_like(acc_k)
    acc_v[...] = jnp.zeros_like(acc_v)
    for tile in range(rows // QTILE):
        low, high = tile * QTILE, (tile + 1) * QTILE
        ctx = jnp.zeros((QTILE, PAIR), F32)
        dq = jnp.zeros((QTILE, PAIR), F32)
        for h in range(2):
            q, g = query_h[h][low:high], grad_h[h][low:high]
            scores = dot_nt(q, keys[:high])
            last = jnp.where(causal, scores[:, low:], -1e30)
            scores = last if tile == 0 else jnp.concatenate([scores[:, :low], last], axis=1)
            peak = jnp.max(scores, axis=1, keepdims=True)
            expo = jnp.exp(scores - peak)
            probs = expo * (1.0 / jnp.sum(expo, axis=1, keepdims=True))
            low_probs = probs.astype(BF16)
            ctx += dot_nn(low_probs, values_h[h][:high])
            grad_probs = dot_nt(g, values[:high])
            inner = jnp.sum(probs * grad_probs, axis=1, keepdims=True)
            grad_scores = (probs * (grad_probs - inner)).astype(BF16)
            dq += dot_nn(grad_scores, keys_h[h][:high])
            acc_k[:high] += dot_tn(grad_scores, q)
            acc_v[:high] += dot_tn(low_probs, g)
        context[0, low:high] = ctx.astype(BF16)
        dq = back(dq * HEAD ** (-0.5), cos[low:high], s1[low:high], s2[low:high])
        gq[0, low:high] = dq.astype(BF16)
    gk[0] = back(acc_k[...], cos, s1, s2).astype(BF16)
    gv[0] = acc_v[...].astype(BF16)


def attention(mixed, grad_context, tables, group, groups):
    batch, rows, width = grad_context.shape
    pairs = width // PAIR
    each = pairs // groups
    start = group * each
    out = jax.ShapeDtypeStruct((batch, rows, each * PAIR), BF16)

    def at(offset):
        return pl.BlockSpec((1, rows, PAIR), lambda b, p: (b, 0, offset + p))

    table = pl.BlockSpec((rows, PAIR), lambda b, p: (0, 0))
    steps = batch * each
    return pl.pallas_call(
        attention_kernel,
        grid=(batch, each),
        in_specs=[at(start), at(pairs + start), at(2 * pairs + start), at(start)] + [table] * 3,
        out_specs=[at(0)] * 4,
        out_shape=[out] * 4,
        scratch_shapes=[pltpu.VMEM((rows, PAIR), F32)] * 2,
        compiler_params=pltpu.CompilerParams(vmem_limit_bytes=VMEM),
        cost_estimate=pl.CostEstimate(
            flops=steps * 24 * rows * rows * PAIR,
            bytes_accessed=steps * rows * PAIR * 22,
            transcendentals=steps * 2 * rows * rows,
        ),
    )(mixed, mixed, mixed, grad_context, *tables)


def reduce_owner(total):
    copies, owners = lax.axis_size("rep"), lax.axis_size("fsdp")
    core = lax.axis_index("rep") % 2
    half = total.shape[0] // (2 * owners)
    columns = total.shape[1]
    parts = total.reshape(owners, 2, half, columns)
    theirs = lax.dynamic_index_in_dim(parts, 1 - core, 1, keepdims=False).astype(BF16)
    mine = lax.dynamic_index_in_dim(parts, core, 1, keepdims=False)
    got = lax.ppermute(theirs, "rep", [(i, i ^ 1) for i in range(copies)])
    pair = (mine + got.astype(F32)).astype(BF16).reshape(owners * half, columns)
    owned = lax.psum_scatter(pair, "fsdp", scatter_dimension=0, tiled=True)
    every = lax.all_gather(owned, "rep", axis=0, tiled=False).astype(F32)
    every = every.reshape(copies // 2, 2, half, columns)
    return jnp.sum(every, axis=0).reshape(2 * half, columns)


def body(
    tokens,
    lengths,
    cotangent,
    mix_weight,
    mix_bias,
    proj_weight,
    proj_bias,
    up_weight,
    up_bias,
    down_weight,
    down_bias,
    gain_attn,
    shift_attn,
    gain_mlp,
    shift_mlp,
):
    owners = lax.axis_size("fsdp")
    batch, rows, width = tokens.shape
    count = batch * rows
    small = (gain_mlp, shift_mlp, up_bias, gain_attn, shift_attn, mix_bias, proj_bias, down_bias)
    sizes = [piece.shape[0] for piece in small]
    packed = lax.all_gather(jnp.concatenate(small), "fsdp", axis=0, tiled=False)
    pieces, at = [], 0
    for size in sizes:
        pieces.append(packed[:, at : at + size].reshape(owners * size))
        at += size
    gain_mlp, shift_mlp, up_bias, gain_attn, shift_attn, mix_bias, proj_bias, down_bias = pieces
    up_full = lax.all_gather(up_weight, "fsdp", axis=0, tiled=True)
    down_full = lax.all_gather(down_weight, "fsdp", axis=0, tiled=True)
    proj_full = lax.all_gather(proj_weight, "fsdp", axis=0, tiled=True)
    mix_full = lax.all_gather(mix_weight, "fsdp", axis=0, tiled=True)

    places = jnp.arange(rows, dtype=jnp.int32)
    valid = (places[None, :] < lengths[:, None]).reshape(count, 1)
    inputs = tokens.reshape(count, width).astype(F32)
    outer = jnp.where(valid, cotangent.reshape(count, width), jnp.zeros((), BF16))
    mean = jnp.mean(inputs, axis=1, keepdims=True)
    centred = inputs - mean
    scale = lax.rsqrt(jnp.mean(centred * centred, axis=1, keepdims=True) + EPS)
    hat = centred * scale
    g_attn, g_mlp = gain_attn.astype(F32), gain_mlp.astype(F32)
    first = (hat * g_attn + shift_attn.astype(F32)).astype(BF16)
    second = (hat * g_mlp + shift_mlp.astype(F32)).astype(BF16)

    active, grad_hidden = mlp_front(second, outer, up_full, up_bias, down_full)
    grad_down = reduce_owner(dot_tn(active, outer))
    grad_up = reduce_owner(dot_tn(second, grad_hidden))
    grad_second = dot_nt(grad_hidden, up_full)
    feed = dot_nn(active, down_full)

    mixed = (dot_nn(first, mix_full) + mix_bias.astype(F32)).reshape(batch, rows, 3 * width)
    grad_context = dot_nt(outer, proj_full).astype(BF16).reshape(batch, rows, width)
    tables = rotary_tables(rows)
    share = width // GROUPS
    contexts, grads, mix_grads = [], [[], [], []], []
    for group in range(GROUPS):
        context, *three = attention(mixed, grad_context, tables, group, GROUPS)
        three = [piece.reshape(count, share) for piece in three]
        contexts.append(context.reshape(count, share))
        for kind in range(3):
            grads[kind].append(three[kind])
        own = reduce_owner(dot_tn(first, jnp.concatenate(three, axis=1)))
        mix_grads.append(own.reshape(-1, 3, share))
    grad_mix = jnp.stack(mix_grads, axis=2).reshape(-1, 3 * width)
    context = jnp.concatenate(contexts, axis=1)
    grad_mixed = jnp.concatenate(grads[0] + grads[1] + grads[2], axis=1)
    grad_proj = reduce_owner(dot_tn(context, outer))
    attend = dot_nn(context, proj_full)
    result = inputs + attend + feed + (proj_bias.astype(F32) + down_bias.astype(F32))
    result = jnp.where(valid, result, 0.0).astype(BF16)
    grad_first = dot_nt(grad_mixed, mix_full)

    pulled = grad_first * g_attn + grad_second * g_mlp
    into = scale * (
        pulled
        - jnp.mean(pulled, axis=1, keepdims=True)
        - hat * jnp.mean(pulled * hat, axis=1, keepdims=True)
    )
    grad_tokens = outer.astype(F32) + into

    def over_rows(array):
        return jnp.sum(array.astype(F32), axis=0)

    vectors = (
        over_rows(grad_second * hat),
        over_rows(grad_second),
        over_rows(grad_hidden),
        over_rows(grad_first * hat),
        over_rows(grad_first),
        over_rows(grad_mixed),
        over_rows(outer),
    )
    sent = jnp.concatenate([piece.reshape(owners, -1) for piece in vectors], axis=1)
    sent = lax.psum_scatter(sent.astype(BF16), "fsdp", scatter_dimension=0, tiled=True)
    owned = jnp.sum(lax.all_gather(sent[0], "rep", axis=0, tiled=False).astype(F32), axis=0)
    pieces, at = [], 0
    for size in sizes[:7]:
        pieces.append(owned[at : at + size])
        at += size
    d_gain_mlp, d_shift_mlp, d_up_bias, d_gain_attn, d_shift_attn, d_mix_bias, d_bias = pieces
    return (
        result.reshape(batch, rows, width),
        grad_tokens.reshape(batch, rows, width),
        grad_mix,
        d_mix_bias,
        grad_proj,
        d_bias,
        grad_up,
        d_up_bias,
        grad_down,
        d_bias,
        d_gain_attn,
        d_shift_attn,
        d_gain_mlp,
        d_shift_mlp,
    )


def solution(mesh):
    in_specs = (
        P(("rep", "fsdp"), None, None),
        P(("rep", "fsdp")),
        P(("rep", "fsdp"), None, None),
        P("fsdp", None),
        P("fsdp"),
        P("fsdp", None),
        P("fsdp"),
        P("fsdp", None),
        P("fsdp"),
        P("fsdp", None),
        P("fsdp"),
        P("fsdp"),
        P("fsdp"),
        P("fsdp"),
        P("fsdp"),
    )
    out_specs = (
        P(("rep", "fsdp"), None, None),
        P(("rep", "fsdp"), None, None),
        P("fsdp", None),
        P("fsdp"),
        P("fsdp", None),
        P("fsdp"),
        P("fsdp", None),
        P("fsdp"),
        P("fsdp", None),
        P("fsdp"),
        P("fsdp"),
        P("fsdp"),
        P("fsdp"),
        P("fsdp"),
    )
    return jax.shard_map(body, mesh=mesh, in_specs=in_specs, out_specs=out_specs, check_vma=False)
```

```python
import math

import jax
import jax.numpy as jnp
from jax import lax
from jax.experimental import pallas as pl
from jax.experimental.pallas import tpu as pltpu
from jax.sharding import PartitionSpec as P

HEADS = 16
HEAD = 64
ROT = 16
PAIR = 2 * HEAD
GROUPS = 2
QTILE = 256
VMEM = 48 * 1024 * 1024
EPS = 1e-05
BASE = 10000.0
F32 = jnp.float32
BF16 = jnp.bfloat16


def dot_nn(a, b):
    return lax.dot_general(a, b, (((1,), (0,)), ((), ())), preferred_element_type=F32)


def dot_nt(a, b):
    return lax.dot_general(a, b, (((1,), (1,)), ((), ())), preferred_element_type=F32)


def dot_tn(a, b):
    return lax.dot_general(a, b, (((0,), (0,)), ((), ())), preferred_element_type=F32)


def rotary_tables(rows):
    half = ROT // 2
    lane = jnp.arange(PAIR, dtype=jnp.int32) % HEAD
    steps = (lane % half).astype(F32) * (2.0 / ROT)
    inverse = jnp.exp(-math.log(BASE) * steps)
    angles = jnp.arange(rows, dtype=F32)[:, None] * inverse[None, :]
    cosines = jnp.where(lane[None] < ROT, jnp.cos(angles), 1.0)
    ahead = jnp.where(lane[None] < half, -jnp.sin(angles), 0.0)
    behind = jnp.where((lane[None] >= half) & (lane[None] < ROT), jnp.sin(angles), 0.0)
    return cosines, ahead, behind


def mlp_kernel(second, outer, up, up_bias, down, active, grad_hidden):
    hidden = dot_nn(second[...], up[...]) + up_bias[...].astype(F32)
    grad_active = dot_nt(outer[...], down[...])
    below = 0.5 + 0.5 * lax.erf(hidden * (0.5**0.5))
    density = jnp.exp(-0.5 * hidden * hidden) * (1.0 / math.sqrt(2.0 * math.pi))
    active[...] = (hidden * below).astype(BF16)
    grad_hidden[...] = (grad_active * (below + hidden * density)).astype(BF16)


def mlp_front(second, outer, up, up_bias, down):
    rows, width = second.shape
    wide = up.shape[1]
    rt, ft = min(512, rows), min(512, wide)
    out = jax.ShapeDtypeStruct((rows, wide), BF16)
    return pl.pallas_call(
        mlp_kernel,
        grid=(wide // ft, rows // rt),
        in_specs=[
            pl.BlockSpec((rt, width), lambda f, r: (r, 0)),
            pl.BlockSpec((rt, width), lambda f, r: (r, 0)),
            pl.BlockSpec((width, ft), lambda f, r: (0, f)),
            pl.BlockSpec((1, ft), lambda f, r: (0, f)),
            pl.BlockSpec((ft, width), lambda f, r: (f, 0)),
        ],
        out_specs=[pl.BlockSpec((rt, ft), lambda f, r: (r, f))] * 2,
        out_shape=[out, out],
        compiler_params=pltpu.CompilerParams(vmem_limit_bytes=VMEM),
        cost_estimate=pl.CostEstimate(
            flops=4 * rows * width * wide,
            bytes_accessed=rows * wide * 4 + width * wide * 4 + rows * width * 32,
            transcendentals=2 * rows * wide,
        ),
    )(second, outer, up, up_bias.reshape(1, wide), down)


def attention_kernel(qin, kin, vin, gin, cosines, ahead, behind, context, gq, gk, gv, acc_k, acc_v):
    rows = qin.shape[1]
    cos, s1, s2 = cosines[...], ahead[...], behind[...]

    def turn(u):
        return u * cos + pltpu.roll(u, PAIR - ROT // 2, 1) * s1 + pltpu.roll(u, ROT // 2, 1) * s2

    def back(u, c, a, b):
        return u * c - pltpu.roll(u, PAIR - ROT // 2, 1) * a - pltpu.roll(u, ROT // 2, 1) * b

    query = (turn(qin[0]) * HEAD ** (-0.5)).astype(BF16)
    keys = turn(kin[0]).astype(BF16)
    values = vin[0].astype(BF16)
    grad = gin[0]
    lane = lax.broadcasted_iota(jnp.int32, (1, PAIR), 1)
    causal = lax.broadcasted_iota(jnp.int32, (QTILE, QTILE), 0) >= lax.broadcasted_iota(
        jnp.int32, (QTILE, QTILE), 1
    )
    zero = jnp.zeros((), BF16)
    halves = [(lane < HEAD), (lane >= HEAD)]
    query_h = [jnp.where(m, query, zero) for m in halves]
    keys_h = [jnp.where(m, keys, zero) for m in halves]
    values_h = [jnp.where(m, values, zero) for m in halves]
    grad_h = [jnp.where(m, grad, zero) for m in halves]
    acc_k[...] = jnp.zeros_like(acc_k)
    acc_v[...] = jnp.zeros_like(acc_v)
    for tile in range(rows // QTILE):
        low, high = tile * QTILE, (tile + 1) * QTILE
        ctx = jnp.zeros((QTILE, PAIR), F32)
        dq = jnp.zeros((QTILE, PAIR), F32)
        for h in range(2):
            q, g = query_h[h][low:high], grad_h[h][low:high]
            scores = dot_nt(q, keys[:high])
            last = jnp.where(causal, scores[:, low:], -1e30)
            scores = last if tile == 0 else jnp.concatenate([scores[:, :low], last], axis=1)
            peak = jnp.max(scores, axis=1, keepdims=True)
            expo = jnp.exp(scores - peak)
            probs = expo * (1.0 / jnp.sum(expo, axis=1, keepdims=True))
            low_probs = probs.astype(BF16)
            ctx += dot_nn(low_probs, values_h[h][:high])
            grad_probs = dot_nt(g, values[:high])
            inner = jnp.sum(probs * grad_probs, axis=1, keepdims=True)
            grad_scores = (probs * (grad_probs - inner)).astype(BF16)
            dq += dot_nn(grad_scores, keys_h[h][:high])
            acc_k[:high] += dot_tn(grad_scores, q)
            acc_v[:high] += dot_tn(low_probs, g)
        context[0, low:high] = ctx.astype(BF16)
        dq = back(dq * HEAD ** (-0.5), cos[low:high], s1[low:high], s2[low:high])
        gq[0, low:high] = dq.astype(BF16)
    gk[0] = back(acc_k[...], cos, s1, s2).astype(BF16)
    gv[0] = acc_v[...].astype(BF16)


def attention(mixed, grad_context, tables, group, groups):
    batch, rows, width = grad_context.shape
    pairs = width // PAIR
    each = pairs // groups
    start = group * each
    out = jax.ShapeDtypeStruct((batch, rows, each * PAIR), BF16)

    def at(offset):
        return pl.BlockSpec((1, rows, PAIR), lambda b, p: (b, 0, offset + p))

    table = pl.BlockSpec((rows, PAIR), lambda b, p: (0, 0))
    steps = batch * each
    return pl.pallas_call(
        attention_kernel,
        grid=(batch, each),
        in_specs=[at(start), at(pairs + start), at(2 * pairs + start), at(start)] + [table] * 3,
        out_specs=[at(0)] * 4,
        out_shape=[out] * 4,
        scratch_shapes=[pltpu.VMEM((rows, PAIR), F32)] * 2,
        compiler_params=pltpu.CompilerParams(vmem_limit_bytes=VMEM),
        cost_estimate=pl.CostEstimate(
            flops=steps * 24 * rows * rows * PAIR,
            bytes_accessed=steps * rows * PAIR * 22,
            transcendentals=steps * 2 * rows * rows,
        ),
    )(mixed, mixed, mixed, grad_context, *tables)


def chip_halves(total):
    copies, owners = lax.axis_size("rep"), lax.axis_size("fsdp")
    core = lax.axis_index("rep") % 2
    half = total.shape[0] // (2 * owners)
    columns = total.shape[1]
    parts = total.reshape(owners, 2, half, columns)
    theirs = lax.dynamic_index_in_dim(parts, 1 - core, 1, keepdims=False).astype(BF16)
    mine = lax.dynamic_index_in_dim(parts, core, 1, keepdims=False)
    got = lax.ppermute(theirs, "rep", [(i, i ^ 1) for i in range(copies)])
    return (mine + got.astype(F32)).astype(BF16).reshape(owners * half, columns)


def reduce_halves(pair):
    copies, columns = lax.axis_size("rep"), pair.shape[1]
    half = pair.shape[0] // lax.axis_size("fsdp")
    owned = lax.psum_scatter(pair, "fsdp", scatter_dimension=0, tiled=True)
    every = lax.all_gather(owned, "rep", axis=0, tiled=False).astype(F32)
    every = every.reshape(copies // 2, 2, half, columns)
    return jnp.sum(every, axis=0).reshape(2 * half, columns)


def reduce_owner(total):
    return reduce_halves(chip_halves(total))


def gather_whole(shard, after=None):
    if after is not None:
        shard, _ = lax.optimization_barrier((shard, after))
    copies, owners = lax.axis_size("rep"), lax.axis_size("fsdp")
    core = lax.axis_index("rep") % 2
    half, columns = shard.shape[0] // 2, shard.shape[1]
    own = lax.dynamic_index_in_dim(shard.reshape(2, half, columns), core, 0, keepdims=False)
    mine = lax.all_gather(own, "fsdp", axis=0, tiled=True)
    got = lax.ppermute(mine, "rep", [(i, i ^ 1) for i in range(copies)])
    mine_parts = mine.reshape(owners, half, columns)
    got_parts = got.reshape(owners, half, columns)
    first = core == 0
    both = jnp.stack(
        [jnp.where(first, mine_parts, got_parts), jnp.where(first, got_parts, mine_parts)], axis=1
    )
    return both.reshape(2 * owners * half, columns), mine


def body(
    tokens,
    lengths,
    cotangent,
    mix_weight,
    mix_bias,
    proj_weight,
    proj_bias,
    up_weight,
    up_bias,
    down_weight,
    down_bias,
    gain_attn,
    shift_attn,
    gain_mlp,
    shift_mlp,
):
    owners = lax.axis_size("fsdp")
    batch, rows, width = tokens.shape
    count = batch * rows
    small = (gain_mlp, shift_mlp, up_bias, gain_attn, shift_attn, mix_bias, proj_bias, down_bias)
    sizes = [piece.shape[0] for piece in small]
    packed = lax.all_gather(jnp.concatenate(small), "fsdp", axis=0, tiled=False)
    pieces, at = [], 0
    for size in sizes:
        pieces.append(packed[:, at : at + size].reshape(owners * size))
        at += size
    gain_mlp, shift_mlp, up_bias, gain_attn, shift_attn, mix_bias, proj_bias, down_bias = pieces
    up_full, done = gather_whole(up_weight)
    down_full, done = gather_whole(down_weight)
    mix_full, done = gather_whole(mix_weight, done)
    proj_full, _ = gather_whole(proj_weight, done)

    places = jnp.arange(rows, dtype=jnp.int32)
    valid = (places[None, :] < lengths[:, None]).reshape(count, 1)
    inputs = tokens.reshape(count, width).astype(F32)
    outer = jnp.where(valid, cotangent.reshape(count, width), jnp.zeros((), BF16))
    mean = jnp.mean(inputs, axis=1, keepdims=True)
    centred = inputs - mean
    scale = lax.rsqrt(jnp.mean(centred * centred, axis=1, keepdims=True) + EPS)
    hat = centred * scale
    g_attn, g_mlp = gain_attn.astype(F32), gain_mlp.astype(F32)
    first = (hat * g_attn + shift_attn.astype(F32)).astype(BF16)
    second = (hat * g_mlp + shift_mlp.astype(F32)).astype(BF16)

    active, grad_hidden = mlp_front(second, outer, up_full, up_bias, down_full)
    half_down = chip_halves(dot_tn(active, outer))
    half_up = chip_halves(dot_tn(second, grad_hidden))
    grad_down, grad_up = reduce_halves(half_down), reduce_halves(half_up)
    grad_second = dot_nt(grad_hidden, up_full)
    feed = dot_nn(active, down_full)

    mixed = (dot_nn(first, mix_full) + mix_bias.astype(F32)).reshape(batch, rows, 3 * width)
    grad_context = dot_nt(outer, proj_full).astype(BF16).reshape(batch, rows, width)
    grad_context, _, _ = lax.optimization_barrier((grad_context, half_down, half_up))
    tables = rotary_tables(rows)
    share = width // GROUPS
    contexts, grads, mix_grads = [], [[], [], []], []
    for group in range(GROUPS):
        context, *three = attention(mixed, grad_context, tables, group, GROUPS)
        three = [piece.reshape(count, share) for piece in three]
        contexts.append(context.reshape(count, share))
        for kind in range(3):
            grads[kind].append(three[kind])
        own = reduce_owner(dot_tn(first, jnp.concatenate(three, axis=1)))
        mix_grads.append(own.reshape(-1, 3, share))
    grad_mix = jnp.stack(mix_grads, axis=2).reshape(-1, 3 * width)
    context = jnp.concatenate(contexts, axis=1)
    grad_mixed = jnp.concatenate(grads[0] + grads[1] + grads[2], axis=1)
    grad_proj = reduce_owner(dot_tn(context, outer))
    attend = dot_nn(context, proj_full)
    result = inputs + attend + feed + (proj_bias.astype(F32) + down_bias.astype(F32))
    result = jnp.where(valid, result, 0.0).astype(BF16)
    grad_first = dot_nt(grad_mixed, mix_full)

    pulled = grad_first * g_attn + grad_second * g_mlp
    into = scale * (
        pulled
        - jnp.mean(pulled, axis=1, keepdims=True)
        - hat * jnp.mean(pulled * hat, axis=1, keepdims=True)
    )
    grad_tokens = outer.astype(F32) + into

    def over_rows(array):
        return jnp.sum(array.astype(F32), axis=0)

    vectors = (
        over_rows(grad_second * hat),
        over_rows(grad_second),
        over_rows(grad_hidden),
        over_rows(grad_first * hat),
        over_rows(grad_first),
        over_rows(grad_mixed),
        over_rows(outer),
    )
    sent = jnp.concatenate([piece.reshape(owners, -1) for piece in vectors], axis=1)
    sent = lax.psum_scatter(sent.astype(BF16), "fsdp", scatter_dimension=0, tiled=True)
    owned = jnp.sum(lax.all_gather(sent[0], "rep", axis=0, tiled=False).astype(F32), axis=0)
    pieces, at = [], 0
    for size in sizes[:7]:
        pieces.append(owned[at : at + size])
        at += size
    d_gain_mlp, d_shift_mlp, d_up_bias, d_gain_attn, d_shift_attn, d_mix_bias, d_bias = pieces
    return (
        result.reshape(batch, rows, width),
        grad_tokens.reshape(batch, rows, width),
        grad_mix,
        d_mix_bias,
        grad_proj,
        d_bias,
        grad_up,
        d_up_bias,
        grad_down,
        d_bias,
        d_gain_attn,
        d_shift_attn,
        d_gain_mlp,
        d_shift_mlp,
    )


def solution(mesh):
    in_specs = (
        P(("rep", "fsdp"), None, None),
        P(("rep", "fsdp")),
        P(("rep", "fsdp"), None, None),
        P("fsdp", None),
        P("fsdp"),
        P("fsdp", None),
        P("fsdp"),
        P("fsdp", None),
        P("fsdp"),
        P("fsdp", None),
        P("fsdp"),
        P("fsdp"),
        P("fsdp"),
        P("fsdp"),
        P("fsdp"),
    )
    out_specs = (
        P(("rep", "fsdp"), None, None),
        P(("rep", "fsdp"), None, None),
        P("fsdp", None),
        P("fsdp"),
        P("fsdp", None),
        P("fsdp"),
        P("fsdp", None),
        P("fsdp"),
        P("fsdp", None),
        P("fsdp"),
        P("fsdp"),
        P("fsdp"),
        P("fsdp"),
        P("fsdp"),
    )
    return jax.shard_map(body, mesh=mesh, in_specs=in_specs, out_specs=out_specs, check_vma=False)
```
